32 devices in a mesh: groups: 1, con: 8 (over z, core), var: 4 (over y, x).
Axes of the slice: x: 2, y: 2, z: 4, core: 2. Of those that a mesh axis runs over, the one named last changes fastest.
Arguments:
- tile_values: bfloat16 [8, 4, 64, 128, 128], P('con', 'var', 'groups'), may hold values from -0.1875 to 0.1875
- tile_row: int32 [8, 4, 64], P('con', 'var', 'groups'), may hold values from 0 to 31
- tile_col: int32 [8, 4, 64], P('con', 'var', 'groups'), may hold values from 0 to 255
- tile_count: int32 [8, 4, 1], P('con', 'var', 'groups'), may hold values from 32 to 64, as said below
- unit_cost: float32 [131072], P(('groups', 'var')), may hold values from -6 to 6
- demand: float32 [8, 32768], P('groups', 'con'), may hold values from -6 to 6
- x_saved: bfloat16 [5, 8, 131072], P(None, 'groups', 'var'), may hold values from 0 to 2
- y_saved: bfloat16 [4, 8, 32768], P(None, 'groups', 'con'), may hold values from 0 to 2
- x_active: int32 [4, 8, 131072], P(None, 'groups', 'var'), may hold values 0 or 1
- y_active: int32 [4, 8, 32768], P(None, 'groups', 'con'), may hold values 0 or 1
- x_cot: float32 [8, 131072], P('groups', 'var'), may hold values from -6 to 6
- y_cot: float32 [8, 32768], P('groups', 'con'), may hold values from -6 to 6
- primal_step: float32 [4], replicated, may hold values from 0.1 to 0.5
- dual_step: float32 [4], replicated, may hold values from 0.1 to 0.5
Outputs:
- x_grad: float32 [8, 131072], P('groups', 'var')
- y_grad: float32 [8, 32768], P('groups', 'con')
- step_grads: float32 [2, 4], P('groups')
The draws below stay inside these ranges and needn't reach their ends.
Inputs may be any that keep to these rules, and one draw needn't show every extreme that they name: `tile_count`: some device uses all 64 slots. `tile_row`: positions may repeat within a device.
All inputs are finite; a program needn't handle non-finite values. No bound on the sum of `x_active` or of `y_active` on one device may be relied on, other than what follows from the above.
Results may differ from the reference program's by a relative error of at most 0.003.
Values may be sent and summed in bfloat16 or wider, within the bound.
A program may use at most 64 MiB of HBM per device.

```python
import math
import jax
import jax.numpy as jnp
from jax import lax

TILE = 128
RT_DEV = 32
CT_DEV = 256
TILES_DEV = 64
RHS = 8
KITER = 4
GRID_ROWS = 8
GRID_COLS = 4
MROWS = 32768
NCOLS = 131072


def draw_tile_count(key, part):
    key = jax.random.fold_in(key, 7)
    first_key, second_key = jax.random.split(key)
    counts = jax.random.randint(first_key, (GRID_ROWS * GRID_COLS,), TILES_DEV // 2, TILES_DEV + 1)
    chosen = jax.random.randint(second_key, (), 0, GRID_ROWS * GRID_COLS)
    counts = jnp.where(jnp.arange(GRID_ROWS * GRID_COLS) == chosen, TILES_DEV, counts)
    return counts.reshape(GRID_ROWS, GRID_COLS, 1).astype(jnp.int32)


def touch_ends(array, rng, smallest, top_value):
    shape = array.shape
    place = [jax.random.randint(jax.random.fold_in(rng, axis), (), 0, shape[axis]) for axis in range(len(shape))]
    array = array.at[tuple(place)].set(smallest)
    longest = shape.index(max(shape))
    place[longest] = (place[longest] + 1) % shape[longest]
    return array.at[tuple(place)].set(top_value)


def shard_levels(key, extent, cuts, least, largest):
    level = 1.0
    for axis_at, blocks in cuts:
        draws = jax.random.uniform(jax.random.fold_in(jax.random.fold_in(key, 6), axis_at), (blocks,), jnp.float32, least / len(cuts), largest / len(cuts))
        level = level * jnp.repeat(jnp.exp(draws), extent[axis_at] // blocks).reshape((-1,) + (1,) * (len(extent) - 1 - axis_at))
    return level


def normal_values(key, shape, scale, limit, pieces=(), dtype=jnp.bfloat16):
    values = jax.random.normal(key, shape, jnp.float32) * scale
    if len(pieces) > 0:
        values = shard_levels(key, shape, pieces, -0.22, 0.18) * values
    return jnp.clip(values, min=-limit, max=limit).astype(dtype)


def setup_inputs(seed: int = 0, part: int = 0) -> dict:
    streams_of = jax.random.split(jax.random.key(seed), 15)
    own_keys = jax.random.split(jax.random.fold_in(streams_of[14], part), 15)
    tile_values = normal_values(own_keys[0], (GRID_ROWS, GRID_COLS, TILES_DEV, TILE, TILE), (TILE * max(1, TILES_DEV * GRID_COLS // RT_DEV)) ** -0.5, 0.1875, ((0, 8), (1, 4)))
    tile_row = touch_ends(jax.random.randint(own_keys[1], (GRID_ROWS, GRID_COLS, TILES_DEV), 0, RT_DEV), jax.random.fold_in(own_keys[1], 1), 0, RT_DEV - 1).astype(jnp.int32)
    tile_col = touch_ends(jax.random.randint(own_keys[2], (GRID_ROWS, GRID_COLS, TILES_DEV), 0, CT_DEV), jax.random.fold_in(own_keys[2], 1), 0, CT_DEV - 1).astype(jnp.int32)
    tile_count = draw_tile_count(jax.random.fold_in(jax.random.fold_in(streams_of[14], part), 71), part)
    unit_cost = normal_values(own_keys[4], (NCOLS,), 1.0, 6.0, ((0, 4),), jnp.float32)
    demand = normal_values(own_keys[5], (RHS, MROWS), 1.0, 6.0, ((1, 8),), jnp.float32)
    x_saved = jnp.clip(2.0 * jax.random.uniform(own_keys[6], (KITER + 1, RHS, NCOLS), jnp.float32) ** shard_levels(own_keys[6], (KITER + 1, RHS, NCOLS), ((2, 4),), -0.2, 0.2), 0.0, 2.0).astype(jnp.bfloat16)
    y_saved = jnp.clip(2.0 * jax.random.uniform(own_keys[7], (KITER, RHS, MROWS), jnp.float32) ** shard_levels(own_keys[7], (KITER, RHS, MROWS), ((2, 8),), -0.2, 0.2), 0.0, 2.0).astype(jnp.bfloat16)
    x_active = touch_ends((jax.random.randint(own_keys[8], (KITER, RHS, NCOLS), 0, 5) < 3).astype(jnp.int32), jax.random.fold_in(own_keys[8], 1), 0, 1)
    y_active = touch_ends((jax.random.randint(own_keys[9], (KITER, RHS, MROWS), 0, 5) < 3).astype(jnp.int32), jax.random.fold_in(own_keys[9], 1), 0, 1)
    x_cot = normal_values(own_keys[10], (RHS, NCOLS), 1.0, 6.0, ((1, 4),), jnp.float32)
    y_cot = normal_values(own_keys[11], (RHS, MROWS), 1.0, 6.0, ((1, 8),), jnp.float32)
    primal_step = jnp.clip(jnp.exp(jax.random.uniform(streams_of[12], (KITER,), jnp.float32, math.log(0.1), math.log(0.5))), 0.1, 0.5)
    dual_step = jnp.clip(jnp.exp(jax.random.uniform(streams_of[13], (KITER,), jnp.float32, math.log(0.1), math.log(0.5))), 0.1, 0.5)
    return {"tile_values": tile_values, "tile_row": tile_row, "tile_col": tile_col, "tile_count": tile_count, "unit_cost": unit_cost, "demand": demand, "x_saved": x_saved, "y_saved": y_saved, "x_active": x_active, "y_active": y_active, "x_cot": x_cot, "y_cot": y_cot, "primal_step": primal_step, "dual_step": dual_step}


def adjoint_apply(tile_values, tile_row, tile_col, valid, vector):
    parts = vector.reshape(RHS, GRID_ROWS, RT_DEV, TILE).transpose(1, 0, 2, 3)
    lanes = jnp.broadcast_to(jnp.arange(GRID_COLS)[:, None], (GRID_COLS, TILES_DEV))

    def one_block(total, items):
        blocks, rows, cols, used, piece = items
        gathered = piece[:, rows, :]
        product = jnp.einsum('jtab,rjta->rjtb', blocks.astype(jnp.float32), gathered.astype(jnp.float32), precision=lax.Precision.HIGHEST)
        product = product * used[None, :, :, None]
        return (total.at[:, lanes, cols, :].add(product), None)
    start = jnp.zeros((RHS, GRID_COLS, CT_DEV, TILE), jnp.float32)
    total, unused = lax.scan(one_block, start, (tile_values, tile_row, tile_col, valid, parts))
    return total.reshape(RHS, NCOLS)

def forward_apply(tile_values, tile_row, tile_col, valid, vector):
    parts = vector.reshape(RHS, GRID_COLS, CT_DEV, TILE)
    lanes = jnp.broadcast_to(jnp.arange(GRID_COLS)[:, None], (GRID_COLS, TILES_DEV))

    def one_block(carry, items):
        blocks, rows, cols, used = items
        gathered = parts[:, lanes, cols, :]
        product = jnp.einsum('jtab,rjtb->rjta', blocks.astype(jnp.float32), gathered.astype(jnp.float32), precision=lax.Precision.HIGHEST)
        product = product * used[None, :, :, None]
        result = jnp.zeros((RHS, RT_DEV, TILE), jnp.float32).at[:, rows, :].add(product)
        return (carry, result)
    unused, outs = lax.scan(one_block, jnp.zeros((), jnp.float32), (tile_values, tile_row, tile_col, valid))
    return outs.transpose(1, 0, 2, 3).reshape(RHS, MROWS)

def reference(tile_values, tile_row, tile_col, tile_count, unit_cost, demand, x_saved, y_saved, x_active, y_active, x_cot, y_cot, primal_step, dual_step):
    valid = (jnp.arange(TILES_DEV)[None, None, :] < tile_count).astype(jnp.float32)
    scale = 1.0 / math.sqrt(RHS * NCOLS)
    x_bar = x_cot
    y_bar = y_cot
    tau_list = []
    sigma_list = []
    for position in reversed(range(KITER)):
        weighted = y_active[position].astype(jnp.float32) * y_bar
        column_part = adjoint_apply(tile_values, tile_row, tile_col, valid, weighted.astype(jnp.bfloat16))
        extrapolated = 2.0 * x_saved[position + 1].astype(jnp.float32) - x_saved[position].astype(jnp.float32)
        sigma_term = scale * jnp.sum(weighted * demand) - scale * jnp.sum(column_part * extrapolated)
        x_bar = x_bar - 2.0 * dual_step[position] * column_part
        masked = x_active[position].astype(jnp.float32) * x_bar
        row_part = forward_apply(tile_values, tile_row, tile_col, valid, masked.astype(jnp.bfloat16))
        tau_term = scale * jnp.sum(row_part * y_saved[position].astype(jnp.float32)) - scale * jnp.sum(masked * unit_cost[None, :])
        y_bar = weighted + primal_step[position] * row_part
        x_bar = masked + dual_step[position] * column_part
        tau_list.append(tau_term)
        sigma_list.append(sigma_term)
    step_grads = jnp.stack([jnp.stack(tau_list[::-1]), jnp.stack(sigma_list[::-1])])
    return (x_bar, y_bar, step_grads)
```

```python
import functools
import math

import jax
import jax.numpy as jnp
from jax import lax
from jax.experimental import pallas as pl
from jax.experimental.pallas import tpu as pltpu
from jax.sharding import PartitionSpec as P

MESH = pl.DeviceIdType.MESH
F32 = jnp.float32
BF16 = jnp.bfloat16


def kernel(
    n_con,
    n_var,
    row_s,
    col_s,
    count_s,
    psteps,
    dsteps,
    row_v,
    col_v,
    blocks,
    cost,
    demand,
    x_saved,
    y_saved,
    x_active,
    y_active,
    x_cot,
    y_cot,
    x_out,
    y_out,
    g_out,
    idx,
    onehot,
    row_onehot,
    prod,
    terms,
    row_terms,
    p_tiles,
    u_tiles,
    s_tiles,
    w_tiles,
    partial,
    g_con,
    g_var,
    idx_send,
    idx_recv,
    con_send,
    con_recv,
    var_send,
    var_recv,
    gc_send,
    gc_recv,
    gv_send,
    gv_recv,
):
    slots, width, _ = blocks.shape
    rhs = x_cot.shape[0]
    col_tiles = x_cot.shape[1] // width
    row_tiles = y_cot.shape[1] // width
    steps = y_active.shape[0]
    chips = n_con // 2
    me = lax.axis_index("con")
    mine = lax.axis_index("var")
    core = lax.rem(me, 2)
    chip = lax.div(me, 2)
    sibling = chip * 2 + 1 - core
    scale = 1.0 / math.sqrt(rhs * x_cot.shape[1] * n_var)
    y_weight = scale / n_var
    x_weight = scale / n_con

    def con_peer(offset):
        return lax.rem(me + offset, n_con)

    def var_peer(offset):
        return lax.rem(mine + offset, n_var)

    def chip_peer(offset):
        return lax.rem(chip + offset, chips) * 2 + core

    def con_copy(ref, send, recv, source, target):
        return pltpu.make_async_remote_copy(
            src_ref=ref.at[source],
            dst_ref=ref.at[source],
            send_sem=send,
            recv_sem=recv.at[source],
            device_id={"con": target},
            device_id_type=MESH,
        )

    def var_copy(ref, send, recv, source, target):
        return pltpu.make_async_remote_copy(
            src_ref=ref.at[source],
            dst_ref=ref.at[source],
            send_sem=send,
            recv_sem=recv.at[source],
            device_id={"var": target},
            device_id_type=MESH,
        )

    barrier = pltpu.get_barrier_semaphore()
    for offset in range(1, n_con):
        pl.semaphore_signal(
            barrier, inc=1, device_id={"con": con_peer(offset)}, device_id_type=MESH
        )
    for offset in range(1, n_var):
        pl.semaphore_signal(
            barrier, inc=1, device_id={"var": var_peer(offset)}, device_id_type=MESH
        )

    count = count_s[0, 0]
    slot_lane = lax.broadcasted_iota(jnp.int32, (1, slots), 1)
    own_cols = jnp.where(slot_lane < count, col_v[...], -1)
    own_rows = jnp.where(slot_lane < count, row_v[...], -1)
    idx[me] = jnp.broadcast_to(
        jnp.concatenate([own_cols, own_cols], axis=1), (8, 2 * slots)
    )
    row_onehot[...] = (
        lax.broadcasted_iota(jnp.int32, (row_tiles, 2 * slots), 0)
        == jnp.concatenate([own_rows, own_rows], axis=1)
    ).astype(F32).astype(BF16)

    def first(c, acc):
        cols = pl.ds(pl.multiple_of(c * width, width), width)
        w = y_active[steps - 1, :, cols].astype(F32) * y_cot[:, cols]
        w_tiles[c] = w
        return acc + w * demand[:, cols]

    w_acc = lax.fori_loop(0, row_tiles, first, jnp.zeros((rhs, width), F32))

    pl.semaphore_wait(barrier, n_con - 1 + n_var - 1)
    for offset in range(1, n_con):
        con_copy(idx, idx_send.at[offset - 1], idx_recv, me, con_peer(offset)).start()

    unroll = 8

    def step(i, w_acc):
        k = steps - 1 - i
        terms_k = terms.at[k]
        row_terms_k = row_terms.at[k]
        con_send_k = con_send.at[k]
        con_recv_k = con_recv.at[k]
        var_send_k = var_send.at[k]
        var_recv_k = var_recv.at[k]
        tau_step = psteps[k]
        sigma_step = dsteps[k]

        def down(g, carry):
            for o in range(unroll):
                t = g * unroll + o
                v = w_tiles[row_s[0, t]].astype(BF16)
                prod[pl.ds(t, rhs, stride=slots), :] = jnp.dot(
                    v, blocks[t], preferred_element_type=F32
                )
            return carry

        lax.fori_loop(0, slots // unroll, down, 0)
        terms_k[me] = prod[...].astype(BF16)
        for offset in range(1, chips):
            con_copy(
                terms_k, con_send_k.at[offset - 1], con_recv_k, me, chip_peer(offset)
            ).start()
        con_copy(terms_k, con_send_k.at[chips - 1], con_recv_k, me, sibling).start()

        @pl.when(i == 0)
        def _():
            for offset in range(1, n_con):
                source = con_peer(offset)
                con_copy(idx, idx_send.at[offset - 1], idx_recv, source, source).wait_recv()
            lane = lax.broadcasted_iota(jnp.int32, (1, 2 * slots), 1)
            for pair in range(chips):
                both = jnp.where(
                    lane < slots, idx[2 * pair, 0:1, :], idx[2 * pair + 1, 0:1, :]
                )
                onehot[:, pl.ds(pair * 2 * slots, 2 * slots)] = (
                    lax.broadcasted_iota(jnp.int32, (col_tiles, 2 * slots), 0) == both
                ).astype(F32).astype(BF16)
            for offset in range(1, n_con):
                con_copy(
                    idx, idx_send.at[offset - 1], idx_recv, me, con_peer(offset)
                ).wait_send()

        for offset in range(1, chips):
            source = chip_peer(offset)
            con_copy(
                terms_k, con_send_k.at[chips + offset - 1], con_recv_k, source, sibling
            ).wait_recv()
            con_copy(
                terms_k, con_send_k.at[chips + offset - 1], con_recv_k, source, sibling
            ).start()
        for offset in range(chips):
            source = lax.rem(chip + offset, chips) * 2 + 1 - core
            con_copy(terms_k, con_send_k.at[0], con_recv_k, source, sibling).wait_recv()

        for r in range(rhs):
            right = jnp.concatenate(
                [terms_k[d, pl.ds(r * slots, slots), :] for d in range(n_con)], axis=0
            )
            p_tiles[pl.ds(r, col_tiles, stride=rhs), :] = jnp.dot(
                onehot[...], right, preferred_element_type=F32
            )

        source_x = x_out

        def columns(g, accs):
            ext_acc, cost_acc = accs
            for o in range(unroll):
                c = g * unroll + o
                cols = pl.ds(pl.multiple_of(c * width, width), width)
                rows = pl.ds(pl.multiple_of(c * rhs, rhs), rhs)
                p = p_tiles[rows, :]
                later = x_saved[k + 1, :, cols].astype(F32)
                earlier = x_saved[k, :, cols].astype(F32)
                ext_acc = ext_acc + p * (2.0 * later - earlier)
                q = x_active[k, :, cols].astype(F32) * (
                    source_x[:, cols] - 2.0 * sigma_step * p
                )
                u_tiles[c] = q
                cost_acc = cost_acc + q * cost[:, cols]
                x_out[:, cols] = q + sigma_step * p
            return ext_acc, cost_acc

        zero = jnp.zeros((rhs, width), F32)
        ext_acc, cost_acc = lax.fori_loop(
            0, col_tiles // unroll, columns, (zero, zero)
        )

        def across(g, carry):
            for o in range(unroll):
                t = g * unroll + o
                u = u_tiles[col_s[0, t]].astype(BF16)
                prod[pl.ds(t, rhs, stride=slots), :] = lax.dot_general(
                    u, blocks[t], (((1,), (1,)), ((), ())), preferred_element_type=F32
                )
            return carry

        lax.fori_loop(0, slots // unroll, across, 0)
        for r in range(rhs):
            slab = prod[pl.ds(r * slots, slots), :]
            high = slab.astype(BF16)
            low = (slab - high.astype(F32)).astype(BF16)
            s_tiles[pl.ds(r, row_tiles, stride=rhs), :] = jnp.dot(
                row_onehot[...],
                jnp.concatenate([high, low], axis=0),
                preferred_element_type=F32,
            )
        row_terms_k[mine] = s_tiles[...].astype(BF16)
        for offset in range(1, n_var):
            var_copy(
                row_terms_k, var_send_k.at[offset - 1], var_recv_k, mine, var_peer(offset)
            ).start()

        def dual_dot(c, acc):
            cols = pl.ds(pl.multiple_of(c * width, width), width)
            rows = pl.ds(pl.multiple_of(c * rhs, rhs), rhs)
            return acc + s_tiles[rows, :] * y_saved[k, :, cols].astype(F32)

        s_acc = lax.fori_loop(0, row_tiles, dual_dot, zero)
        partial[pl.ds(k, 1), :] = jnp.sum(
            scale * s_acc - x_weight * cost_acc, axis=0, keepdims=True
        )
        partial[pl.ds(steps + k, 1), :] = jnp.sum(
            y_weight * w_acc - x_weight * ext_acc, axis=0, keepdims=True
        )

        for offset in range(1, n_var):
            source = var_peer(offset)
            var_copy(
                row_terms_k, var_send_k.at[offset - 1], var_recv_k, source, source
            ).wait_recv()
        total = row_terms_k[0].astype(F32)
        for j in range(1, n_var):
            total = total + row_terms_k[j].astype(F32)
        s_tiles[...] = total
        before = jnp.maximum(k - 1, 0)

        def rows_loop(c, acc):
            cols = pl.ds(pl.multiple_of(c * width, width), width)
            rows = pl.ds(pl.multiple_of(c * rhs, rhs), rhs)
            y_bar = w_tiles[c] + tau_step * s_tiles[rows, :]
            y_out[:, cols] = y_bar
            w = y_active[before, :, cols].astype(F32) * y_bar
            w_tiles[c] = w
            return acc + w * demand[:, cols]

        w_acc = lax.fori_loop(0, row_tiles, rows_loop, zero)

        for offset in range(2 * chips - 1):
            con_copy(terms_k, con_send_k.at[offset], con_recv_k, me, sibling).wait_send()
        for offset in range(1, n_var):
            var_copy(
                row_terms_k, var_send_k.at[offset - 1], var_recv_k, mine, var_peer(offset)
            ).wait_send()
        return w_acc

    x_out[...] = x_cot[...]
    lax.fori_loop(0, steps, step, w_acc)

    g_con[me] = partial[...]
    for offset in range(1, n_con):
        con_copy(g_con, gc_send.at[offset - 1], gc_recv, me, con_peer(offset)).start()
    for offset in range(1, n_con):
        source = con_peer(offset)
        con_copy(g_con, gc_send.at[offset - 1], gc_recv, source, source).wait_recv()
    sums = g_con[0]
    for d in range(1, n_con):
        sums = sums + g_con[d]
    g_var[mine] = sums
    for offset in range(1, n_var):
        var_copy(g_var, gv_send.at[offset - 1], gv_recv, mine, var_peer(offset)).start()
    for offset in range(1, n_var):
        source = var_peer(offset)
        var_copy(g_var, gv_send.at[offset - 1], gv_recv, source, source).wait_recv()
    sums = g_var[0]
    for j in range(1, n_var):
        sums = sums + g_var[j]
    for n in range(2 * steps):
        g_out[n // steps, n % steps] = jnp.sum(sums[n : n + 1, :])
    for offset in range(1, n_con):
        con_copy(g_con, gc_send.at[offset - 1], gc_recv, me, con_peer(offset)).wait_send()
    for offset in range(1, n_var):
        var_copy(g_var, gv_send.at[offset - 1], gv_recv, mine, var_peer(offset)).wait_send()


def per_device(
    tile_values,
    tile_row,
    tile_col,
    tile_count,
    unit_cost,
    demand,
    x_saved,
    y_saved,
    x_active,
    y_active,
    x_cot,
    y_cot,
    primal_step,
    dual_step,
):
    blocks = tile_values.reshape(tile_values.shape[2:])
    slots, width, _ = blocks.shape
    rhs = x_cot.shape[0]
    col_tiles = x_cot.shape[1] // width
    row_tiles = y_cot.shape[1] // width
    steps = primal_step.shape[0]
    n_con = lax.axis_size("con")
    n_var = lax.axis_size("var")
    chips = n_con // 2
    rows = tile_row.reshape(1, slots)
    cols = tile_col.reshape(1, slots)
    vmem = pl.BlockSpec(memory_space=pltpu.VMEM)
    smem = pl.BlockSpec(memory_space=pltpu.SMEM)
    dma = pltpu.SemaphoreType.DMA
    return pl.pallas_call(
        functools.partial(kernel, n_con, n_var),
        out_shape=(
            jax.ShapeDtypeStruct(x_cot.shape, F32),
            jax.ShapeDtypeStruct(y_cot.shape, F32),
            jax.ShapeDtypeStruct((2, steps), F32),
        ),
        in_specs=[smem] * 5 + [vmem] * 11,
        out_specs=(vmem, vmem, smem),
        scratch_shapes=[
            pltpu.VMEM((n_con, 8, 2 * slots), jnp.int32),
            pltpu.VMEM((col_tiles, n_con * slots), BF16),
            pltpu.VMEM((row_tiles, 2 * slots), BF16),
            pltpu.VMEM((rhs * slots, width), F32),
            pltpu.VMEM((steps, n_con, rhs * slots, width), BF16),
            pltpu.VMEM((steps, n_var, rhs * row_tiles, width), BF16),
            pltpu.VMEM((rhs * col_tiles, width), F32),
            pltpu.VMEM((col_tiles, rhs, width), F32),
            pltpu.VMEM((rhs * row_tiles, width), F32),
            pltpu.VMEM((row_tiles, rhs, width), F32),
            pltpu.VMEM((2 * steps, width), F32),
            pltpu.VMEM((n_con, 2 * steps, width), F32),
            pltpu.VMEM((n_var, 2 * steps, width), F32),
            dma((n_con - 1,)),
            dma((n_con,)),
            dma((steps, 2 * chips - 1)),
            dma((steps, n_con)),
            dma((steps, n_var - 1)),
            dma((steps, n_var)),
            dma((n_con - 1,)),
            dma((n_con,)),
            dma((n_var - 1,)),
            dma((n_var,)),
        ],
        compiler_params=pltpu.CompilerParams(
            collective_id=0, has_side_effects=True, vmem_limit_bytes=56 * 1024 * 1024
        ),
    )(
        rows,
        cols,
        tile_count.reshape(1, 1),
        primal_step,
        dual_step,
        rows,
        cols,
        blocks,
        unit_cost.reshape(1, unit_cost.shape[0]),
        demand,
        x_saved,
        y_saved,
        x_active,
        y_active,
        x_cot,
        y_cot,
    )


def solution(mesh):
    in_specs = (
        P("con", "var", "groups", None, None),
        P("con", "var", "groups"),
        P("con", "var", "groups"),
        P("con", "var", "groups"),
        P(("groups", "var")),
        P("groups", "con"),
        P(None, "groups", "var"),
        P(None, "groups", "con"),
        P(None, "groups", "var"),
        P(None, "groups", "con"),
        P("groups", "var"),
        P("groups", "con"),
        P(),
        P(),
    )
    out_specs = (P("groups", "var"), P("groups", "con"), P("groups", None))
    return jax.shard_map(
        per_device, mesh=mesh, in_specs=in_specs, out_specs=out_specs, check_vma=False
    )
```

```python
import functools
import math

import jax
import jax.numpy as jnp
from jax import lax
from jax.experimental import pallas as pl
from jax.experimental.pallas import tpu as pltpu
from jax.sharding import PartitionSpec as P

MESH = pl.DeviceIdType.MESH
F32 = jnp.float32
BF16 = jnp.bfloat16
PIECES = 4


def kernel(
    n_con,
    n_var,
    row_s,
    col_s,
    count_s,
    psteps,
    dsteps,
    row_v,
    col_v,
    blocks_hbm,
    cost_hbm,
    demand,
    x_saved_hbm,
    y_saved,
    x_active_hbm,
    y_active,
    x_cot_hbm,
    y_cot,
    x_hbm,
    y_out,
    g_out,
    blocks,
    cost,
    x_saved,
    x_active,
    x_out,
    load_sem,
    saved_sem,
    active_sem,
    store_sem,
    idx,
    onehot,
    row_onehot,
    prod,
    terms,
    row_terms,
    p_tiles,
    u_tiles,
    s_tiles,
    w_tiles,
    partial,
    g_con,
    g_var,
    idx_send,
    idx_recv,
    con_send,
    con_recv,
    var_send,
    var_recv,
    gc_send,
    gc_recv,
    gv_send,
    gv_recv,
):
    slots, width, _ = blocks.shape
    rhs = x_out.shape[0]
    col_tiles = x_out.shape[1] // width
    row_tiles = y_cot.shape[1] // width
    steps = y_active.shape[0]
    chips = n_con // 2
    piece = rhs * slots // PIECES
    me = lax.axis_index("con")
    mine = lax.axis_index("var")
    core = lax.rem(me, 2)
    chip = lax.div(me, 2)
    sibling = chip * 2 + 1 - core
    scale = 1.0 / math.sqrt(rhs * x_out.shape[1] * n_var)
    y_weight = scale / n_var
    x_weight = scale / n_con

    def load(source, target, sem):
        return pltpu.make_async_copy(source, target, sem)

    def load_saved(k):
        return load(x_saved_hbm.at[k], x_saved.at[k], saved_sem.at[k])

    def load_active(k):
        return load(x_active_hbm.at[k], x_active.at[k], active_sem.at[k])

    load_blocks = load(blocks_hbm, blocks, load_sem.at[0])
    load_cot = load(x_cot_hbm, x_out, load_sem.at[1])
    load_cost = load(cost_hbm, cost, load_sem.at[2])
    store_x = load(x_out, x_hbm, store_sem.at[0])
    load_blocks.start()
    load_saved(steps).start()
    load_cot.start()
    load_cost.start()
    for k in reversed(range(steps)):
        load_saved(k).start()
        load_active(k).start()

    def con_peer(offset):
        return lax.rem(me + offset, n_con)

    def var_peer(offset):
        return lax.rem(mine + offset, n_var)

    def con_copy(ref, send, recv, source, target):
        return pltpu.make_async_remote_copy(
            src_ref=ref.at[source],
            dst_ref=ref.at[source],
            send_sem=send,
            recv_sem=recv.at[source],
            device_id={"con": target},
            device_id_type=MESH,
        )

    def var_copy(ref, send, recv, source, target):
        return pltpu.make_async_remote_copy(
            src_ref=ref.at[source],
            dst_ref=ref.at[source],
            send_sem=send,
            recv_sem=recv.at[source],
            device_id={"var": target},
            device_id_type=MESH,
        )

    def chain_copy(k, source, part, way):
        target = (me + 2, me - 2, sibling)[way]
        span = pl.ds(part * piece, piece)
        owner = source * 2 + core
        return pltpu.make_async_remote_copy(
            src_ref=terms.at[k, owner, span],
            dst_ref=terms.at[k, owner, span],
            send_sem=con_send.at[k, source, part, way],
            recv_sem=con_recv.at[k, owner, part],
            device_id={"con": target},
            device_id_type=MESH,
        )

    def arrived(k, owner, part):
        span = pl.ds(part * piece, piece)
        pltpu.make_async_remote_copy(
            src_ref=terms.at[k, owner, span],
            dst_ref=terms.at[k, owner, span],
            send_sem=con_send.at[k, 0, part, 0],
            recv_sem=con_recv.at[k, owner, part],
            device_id={"con": sibling},
            device_id_type=MESH,
        ).wait_recv()

    barrier = pltpu.get_barrier_semaphore()
    for offset in range(1, n_con):
        pl.semaphore_signal(
            barrier, inc=1, device_id={"con": con_peer(offset)}, device_id_type=MESH
        )
    for offset in range(1, n_var):
        pl.semaphore_signal(
            barrier, inc=1, device_id={"var": var_peer(offset)}, device_id_type=MESH
        )

    count = count_s[0, 0]
    slot_lane = lax.broadcasted_iota(jnp.int32, (1, slots), 1)
    own_cols = jnp.where(slot_lane < count, col_v[...], -1)
    own_rows = jnp.where(slot_lane < count, row_v[...], -1)
    idx[me] = jnp.broadcast_to(
        jnp.concatenate([own_cols, own_cols], axis=1), (8, 2 * slots)
    )
    row_onehot[...] = (
        lax.broadcasted_iota(jnp.int32, (row_tiles, 2 * slots), 0)
        == jnp.concatenate([own_rows, own_rows], axis=1)
    ).astype(F32).astype(BF16)

    def first(c, acc):
        cols = pl.ds(pl.multiple_of(c * width, width), width)
        w = y_active[steps - 1, :, cols].astype(F32) * y_cot[:, cols]
        w_tiles[c] = w
        return acc + w * demand[:, cols]

    w_acc = lax.fori_loop(0, row_tiles, first, jnp.zeros((rhs, width), F32))

    pl.semaphore_wait(barrier, n_con - 1 + n_var - 1)
    for offset in range(1, n_con):
        con_copy(idx, idx_send.at[offset - 1], idx_recv, me, con_peer(offset)).start()

    unroll = 8

    def step(i, w_acc):
        k = steps - 1 - i
        terms_k = terms.at[k]
        row_terms_k = row_terms.at[k]
        var_send_k = var_send.at[k]
        var_recv_k = var_recv.at[k]
        tau_step = psteps[k]
        sigma_step = dsteps[k]

        def down(g, carry):
            for o in range(unroll):
                t = g * unroll + o
                v = w_tiles[row_s[0, t]].astype(BF16)
                prod[pl.ds(t, rhs, stride=slots), :] = jnp.dot(
                    v, blocks[t], preferred_element_type=F32
                )
            return carry

        lax.fori_loop(0, slots // unroll, down, 0)
        terms_k[me] = prod[...].astype(BF16)
        for part in range(PIECES):

            @pl.when(chip < chips - 1)
            def _():
                chain_copy(k, chip, part, 0).start()

            @pl.when(chip > 0)
            def _():
                chain_copy(k, chip, part, 1).start()

        for part in range(PIECES):
            chain_copy(k, chip, part, 2).start()

        @pl.when(i == 0)
        def _():
            for offset in range(1, n_con):
                source = con_peer(offset)
                con_copy(idx, idx_send.at[offset - 1], idx_recv, source, source).wait_recv()
            lane = lax.broadcasted_iota(jnp.int32, (1, 2 * slots), 1)
            for pair in range(chips):
                both = jnp.where(
                    lane < slots, idx[2 * pair, 0:1, :], idx[2 * pair + 1, 0:1, :]
                )
                onehot[:, pl.ds(pair * 2 * slots, 2 * slots)] = (
                    lax.broadcasted_iota(jnp.int32, (col_tiles, 2 * slots), 0) == both
                ).astype(F32).astype(BF16)
            for offset in range(1, n_con):
                con_copy(
                    idx, idx_send.at[offset - 1], idx_recv, me, con_peer(offset)
                ).wait_send()

        for hop in range(1, chips):
            for part in range(PIECES):

                @pl.when(chip >= hop)
                def _():
                    arrived(k, me - 2 * hop, part)

                    @pl.when(chip < chips - 1)
                    def _():
                        chain_copy(k, chip - hop, part, 0).start()

                    chain_copy(k, chip - hop, part, 2).start()

                @pl.when(chip + hop < chips)
                def _():
                    arrived(k, me + 2 * hop, part)

                    @pl.when(chip > 0)
                    def _():
                        chain_copy(k, chip + hop, part, 1).start()

                    chain_copy(k, chip + hop, part, 2).start()

        for source in range(chips):
            for part in range(PIECES):
                arrived(k, source * 2 + 1 - core, part)

        @pl.when(i == 0)
        def _():
            load_saved(steps).wait()
            load_cot.wait()
            load_cost.wait()

        load_saved(k).wait()
        load_active(k).wait()

        for r in range(rhs):
            right = jnp.concatenate(
                [terms_k[d, pl.ds(r * slots, slots), :] for d in range(n_con)], axis=0
            )
            p_tiles[pl.ds(r, col_tiles, stride=rhs), :] = jnp.dot(
                onehot[...], right, preferred_element_type=F32
            )

        def columns(g, accs):
            ext_acc, cost_acc = accs
            for o in range(unroll):
                c = g * unroll + o
                cols = pl.ds(pl.multiple_of(c * width, width), width)
                rows = pl.ds(pl.multiple_of(c * rhs, rhs), rhs)
                p = p_tiles[rows, :]
                later = x_saved[k + 1, :, cols].astype(F32)
                earlier = x_saved[k, :, cols].astype(F32)
                ext_acc = ext_acc + p * (2.0 * later - earlier)
                q = x_active[k, :, cols].astype(F32) * (
                    x_out[:, cols] - 2.0 * sigma_step * p
                )
                u_tiles[c] = q
                cost_acc = cost_acc + q * cost[:, cols]
                x_out[:, cols] = q + sigma_step * p
            return ext_acc, cost_acc

        zero = jnp.zeros((rhs, width), F32)
        ext_acc, cost_acc = lax.fori_loop(
            0, col_tiles // unroll, columns, (zero, zero)
        )

        @pl.when(k == 0)
        def _():
            store_x.start()

        def across(g, carry):
            for o in range(unroll):
                t = g * unroll + o
                u = u_tiles[col_s[0, t]].astype(BF16)
                prod[pl.ds(t, rhs, stride=slots), :] = lax.dot_general(
                    u, blocks[t], (((1,), (1,)), ((), ())), preferred_element_type=F32
                )
            return carry

        lax.fori_loop(0, slots // unroll, across, 0)
        for r in range(rhs):
            slab = prod[pl.ds(r * slots, slots), :]
            high = slab.astype(BF16)
            low = (slab - high.astype(F32)).astype(BF16)
            s_tiles[pl.ds(r, row_tiles, stride=rhs), :] = jnp.dot(
                row_onehot[...],
                jnp.concatenate([high, low], axis=0),
                preferred_element_type=F32,
            )
        row_terms_k[mine] = s_tiles[...].astype(BF16)
        for offset in range(1, n_var):
            var_copy(
                row_terms_k, var_send_k.at[offset - 1], var_recv_k, mine, var_peer(offset)
            ).start()

        def dual_dot(c, acc):
            cols = pl.ds(pl.multiple_of(c * width, width), width)
            rows = pl.ds(pl.multiple_of(c * rhs, rhs), rhs)
            return acc + s_tiles[rows, :] * y_saved[k, :, cols].astype(F32)

        s_acc = lax.fori_loop(0, row_tiles, dual_dot, zero)
        partial[pl.ds(k, 1), :] = jnp.sum(
            scale * s_acc - x_weight * cost_acc, axis=0, keepdims=True
        )
        partial[pl.ds(steps + k, 1), :] = jnp.sum(
            y_weight * w_acc - x_weight * ext_acc, axis=0, keepdims=True
        )

        @pl.when(k == 0)
        def _():
            g_con[me] = partial[...]
            for offset in range(1, n_con):
                con_copy(
                    g_con, gc_send.at[offset - 1], gc_recv, me, con_peer(offset)
                ).start()

        for offset in range(1, n_var):
            source = var_peer(offset)
            var_copy(
                row_terms_k, var_send_k.at[offset - 1], var_recv_k, source, source
            ).wait_recv()
        total = row_terms_k[0].astype(F32)
        for j in range(1, n_var):
            total = total + row_terms_k[j].astype(F32)
        s_tiles[...] = total
        before = jnp.maximum(k - 1, 0)

        def rows_loop(c, acc):
            cols = pl.ds(pl.multiple_of(c * width, width), width)
            rows = pl.ds(pl.multiple_of(c * rhs, rhs), rhs)
            y_bar = w_tiles[c] + tau_step * s_tiles[rows, :]
            y_out[:, cols] = y_bar
            w = y_active[before, :, cols].astype(F32) * y_bar
            w_tiles[c] = w
            return acc + w * demand[:, cols]

        w_acc = lax.fori_loop(0, row_tiles, rows_loop, zero)

        for source in range(chips):
            for part in range(PIECES):

                @pl.when(jnp.logical_and(source <= chip, chip < chips - 1))
                def _():
                    chain_copy(k, source, part, 0).wait_send()

                @pl.when(jnp.logical_and(source >= chip, chip > 0))
                def _():
                    chain_copy(k, source, part, 1).wait_send()

                chain_copy(k, source, part, 2).wait_send()

        for offset in range(1, n_var):
            var_copy(
                row_terms_k, var_send_k.at[offset - 1], var_recv_k, mine, var_peer(offset)
            ).wait_send()
        return w_acc

    load_blocks.wait()
    lax.fori_loop(0, steps, step, w_acc)

    for offset in range(1, n_con):
        source = con_peer(offset)
        con_copy(g_con, gc_send.at[offset - 1], gc_recv, source, source).wait_recv()
    sums = g_con[0]
    for d in range(1, n_con):
        sums = sums + g_con[d]
    g_var[mine] = sums
    for offset in range(1, n_var):
        var_copy(g_var, gv_send.at[offset - 1], gv_recv, mine, var_peer(offset)).start()
    for offset in range(1, n_var):
        source = var_peer(offset)
        var_copy(g_var, gv_send.at[offset - 1], gv_recv, source, source).wait_recv()
    sums = g_var[0]
    for j in range(1, n_var):
        sums = sums + g_var[j]
    for n in range(2 * steps):
        g_out[n // steps, n % steps] = jnp.sum(sums[n : n + 1, :])
    for offset in range(1, n_con):
        con_copy(g_con, gc_send.at[offset - 1], gc_recv, me, con_peer(offset)).wait_send()
    for offset in range(1, n_var):
        var_copy(g_var, gv_send.at[offset - 1], gv_recv, mine, var_peer(offset)).wait_send()
    store_x.wait()


def per_device(
    tile_values,
    tile_row,
    tile_col,
    tile_count,
    unit_cost,
    demand,
    x_saved,
    y_saved,
    x_active,
    y_active,
    x_cot,
    y_cot,
    primal_step,
    dual_step,
):
    blocks = tile_values.reshape(tile_values.shape[2:])
    slots, width, _ = blocks.shape
    rhs = x_cot.shape[0]
    col_tiles = x_cot.shape[1] // width
    row_tiles = y_cot.shape[1] // width
    steps = primal_step.shape[0]
    n_con = lax.axis_size("con")
    n_var = lax.axis_size("var")
    chips = n_con // 2
    rows = tile_row.reshape(1, slots)
    cols = tile_col.reshape(1, slots)
    vmem = pl.BlockSpec(memory_space=pltpu.VMEM)
    smem = pl.BlockSpec(memory_space=pltpu.SMEM)
    hbm = pl.BlockSpec(memory_space=pl.ANY)
    dma = pltpu.SemaphoreType.DMA
    return pl.pallas_call(
        functools.partial(kernel, n_con, n_var),
        out_shape=(
            jax.ShapeDtypeStruct(x_cot.shape, F32),
            jax.ShapeDtypeStruct(y_cot.shape, F32),
            jax.ShapeDtypeStruct((2, steps), F32),
        ),
        in_specs=[smem] * 5
        + [vmem, vmem, hbm, hbm, vmem, hbm, vmem, hbm, vmem, hbm, vmem],
        out_specs=(hbm, vmem, smem),
        scratch_shapes=[
            pltpu.VMEM((slots, width, width), BF16),
            pltpu.VMEM((1, x_cot.shape[1]), F32),
            pltpu.VMEM(x_saved.shape, BF16),
            pltpu.VMEM(x_active.shape, jnp.int32),
            pltpu.VMEM(x_cot.shape, F32),
            dma((3,)),
            dma((steps + 1,)),
            dma((steps,)),
            dma((1,)),
            pltpu.VMEM((n_con, 8, 2 * slots), jnp.int32),
            pltpu.VMEM((col_tiles, n_con * slots), BF16),
            pltpu.VMEM((row_tiles, 2 * slots), BF16),
            pltpu.VMEM((rhs * slots, width), F32),
            pltpu.VMEM((steps, n_con, rhs * slots, width), BF16),
            pltpu.VMEM((steps, n_var, rhs * row_tiles, width), BF16),
            pltpu.VMEM((rhs * col_tiles, width), F32),
            pltpu.VMEM((col_tiles, rhs, width), F32),
            pltpu.VMEM((rhs * row_tiles, width), F32),
            pltpu.VMEM((row_tiles, rhs, width), F32),
            pltpu.VMEM((2 * steps, width), F32),
            pltpu.VMEM((n_con, 2 * steps, width), F32),
            pltpu.VMEM((n_var, 2 * steps, width), F32),
            dma((n_con - 1,)),
            dma((n_con,)),
            dma((steps, chips, PIECES, 3)),
            dma((steps, n_con, PIECES)),
            dma((steps, n_var - 1)),
            dma((steps, n_var)),
            dma((n_con - 1,)),
            dma((n_con,)),
            dma((n_var - 1,)),
            dma((n_var,)),
        ],
        compiler_params=pltpu.CompilerParams(
            collective_id=0, has_side_effects=True, vmem_limit_bytes=56 * 1024 * 1024
        ),
    )(
        rows,
        cols,
        tile_count.reshape(1, 1),
        primal_step,
        dual_step,
        rows,
        cols,
        blocks,
        unit_cost.reshape(1, unit_cost.shape[0]),
        demand,
        x_saved,
        y_saved,
        x_active,
        y_active,
        x_cot,
        y_cot,
    )


def solution(mesh):
    in_specs = (
        P("con", "var", "groups", None, None),
        P("con", "var", "groups"),
        P("con", "var", "groups"),
        P("con", "var", "groups"),
        P(("groups", "var")),
        P("groups", "con"),
        P(None, "groups", "var"),
        P(None, "groups", "con"),
        P(None, "groups", "var"),
        P(None, "groups", "con"),
        P("groups", "var"),
        P("groups", "con"),
        P(),
        P(),
    )
    out_specs = (P("groups", "var"), P("groups", "con"), P("groups", None))
    return jax.shard_map(
        per_device, mesh=mesh, in_specs=in_specs, out_specs=out_specs, check_vma=False
    )
```

```python
import functools
import math

import jax
import jax.numpy as jnp
from jax import lax
from jax.experimental import pallas as pl
from jax.experimental.pallas import tpu as pltpu
from jax.sharding import PartitionSpec as P

MESH = pl.DeviceIdType.MESH
F32 = jnp.float32
BF16 = jnp.bfloat16
PIECES = 4


def kernel(
    n_con,
    n_var,
    row_s,
    col_s,
    count_s,
    psteps,
    dsteps,
    row_v,
    col_v,
    blocks_hbm,
    cost_hbm,
    demand,
    x_saved_hbm,
    y_saved,
    x_active_hbm,
    y_active,
    x_cot_hbm,
    y_cot,
    x_hbm,
    y_out,
    g_out,
    blocks,
    cost,
    x_saved,
    x_active,
    x_out,
    load_sem,
    saved_sem,
    active_sem,
    store_sem,
    idx,
    onehot,
    row_onehot,
    prod,
    terms,
    row_terms,
    p_tiles,
    u_tiles,
    s_tiles,
    w_tiles,
    partial,
    g_con,
    g_var,
    idx_send,
    idx_recv,
    con_send,
    con_recv,
    var_send,
    var_recv,
    gc_send,
    gc_recv,
    gv_send,
    gv_recv,
):
    slots, width, _ = blocks.shape
    rhs = x_out.shape[0]
    col_tiles = x_out.shape[1] // width
    row_tiles = y_cot.shape[1] // width
    steps = y_active.shape[0]
    chips = n_con // 2
    piece = rhs * slots // PIECES
    me = lax.axis_index("con")
    mine = lax.axis_index("var")
    core = lax.rem(me, 2)
    chip = lax.div(me, 2)
    sibling = chip * 2 + 1 - core
    scale = 1.0 / math.sqrt(rhs * x_out.shape[1] * n_var)
    y_weight = scale / n_var
    x_weight = scale / n_con

    def load(source, target, sem):
        return pltpu.make_async_copy(source, target, sem)

    def load_saved(k):
        return load(x_saved_hbm.at[k], x_saved.at[k], saved_sem.at[k])

    def load_active(k):
        return load(x_active_hbm.at[k], x_active.at[k], active_sem.at[k])

    load_blocks = load(blocks_hbm, blocks, load_sem.at[0])
    load_cot = load(x_cot_hbm, x_out, load_sem.at[1])
    load_cost = load(cost_hbm, cost, load_sem.at[2])
    store_x = load(x_out, x_hbm, store_sem.at[0])
    load_blocks.start()
    load_saved(steps).start()
    load_cot.start()
    load_cost.start()
    for k in reversed(range(steps)):
        load_saved(k).start()
        load_active(k).start()

    def con_peer(offset):
        return lax.rem(me + offset, n_con)

    def var_peer(offset):
        return lax.rem(mine + offset, n_var)

    def con_copy(ref, send, recv, source, target):
        return pltpu.make_async_remote_copy(
            src_ref=ref.at[source],
            dst_ref=ref.at[source],
            send_sem=send,
            recv_sem=recv.at[source],
            device_id={"con": target},
            device_id_type=MESH,
        )

    def var_copy(ref, send, recv, source, target):
        return pltpu.make_async_remote_copy(
            src_ref=ref.at[source],
            dst_ref=ref.at[source],
            send_sem=send,
            recv_sem=recv.at[source],
            device_id={"var": target},
            device_id_type=MESH,
        )

    def chain_copy(k, source, part, way):
        target = (me + 2, me - 2, sibling)[way]
        span = pl.ds(part * piece, piece)
        owner = source * 2 + core
        return pltpu.make_async_remote_copy(
            src_ref=terms.at[k, owner, span],
            dst_ref=terms.at[k, owner, span],
            send_sem=con_send.at[k, source, part, way],
            recv_sem=con_recv.at[k, owner, part],
            device_id={"con": target},
            device_id_type=MESH,
        )

    def arrived(k, owner, part):
        span = pl.ds(part * piece, piece)
        pltpu.make_async_remote_copy(
            src_ref=terms.at[k, owner, span],
            dst_ref=terms.at[k, owner, span],
            send_sem=con_send.at[k, 0, part, 0],
            recv_sem=con_recv.at[k, owner, part],
            device_id={"con": sibling},
            device_id_type=MESH,
        ).wait_recv()

    barrier = pltpu.get_barrier_semaphore()
    for offset in range(1, n_con):
        pl.semaphore_signal(
            barrier, inc=1, device_id={"con": con_peer(offset)}, device_id_type=MESH
        )
    for offset in range(1, n_var):
        pl.semaphore_signal(
            barrier, inc=1, device_id={"var": var_peer(offset)}, device_id_type=MESH
        )

    count = count_s[0, 0]
    slot_lane = lax.broadcasted_iota(jnp.int32, (1, slots), 1)
    own_cols = jnp.where(slot_lane < count, col_v[...], -1)
    own_rows = jnp.where(slot_lane < count, row_v[...], -1)
    idx[me] = jnp.broadcast_to(
        jnp.concatenate([own_cols, own_cols], axis=1), (8, 2 * slots)
    )
    row_onehot[...] = (
        lax.broadcasted_iota(jnp.int32, (row_tiles, 2 * slots), 0)
        == jnp.concatenate([own_rows, own_rows], axis=1)
    ).astype(F32).astype(BF16)

    def first(c, acc):
        cols = pl.ds(pl.multiple_of(c * width, width), width)
        w = y_active[steps - 1, :, cols].astype(F32) * y_cot[:, cols]
        w_tiles[c] = w
        return acc + w * demand[:, cols]

    w_acc = lax.fori_loop(0, row_tiles, first, jnp.zeros((rhs, width), F32), unroll=8)

    pl.semaphore_wait(barrier, n_con - 1 + n_var - 1)
    for offset in range(1, n_con):
        con_copy(idx, idx_send.at[offset - 1], idx_recv, me, con_peer(offset)).start()

    unroll = 8
    group = slots // PIECES
    zeros = jnp.zeros((rhs, width), F32)

    def diagonal(one, two):
        return jnp.concatenate(
            [
                jnp.concatenate([one, zeros], axis=1),
                jnp.concatenate([zeros, two], axis=1),
            ],
            axis=0,
        ).astype(BF16)

    def pair_row(t, part):
        return part * piece + t - part * group

    def keep(row, both):
        prod[pl.ds(row, rhs, stride=group), :] = both[:rhs]
        prod[pl.ds(row + 1, rhs, stride=group), :] = both[rhs:]

    def step(i, w_acc):
        k = steps - 1 - i
        terms_k = terms.at[k]
        row_terms_k = row_terms.at[k]
        var_send_k = var_send.at[k]
        var_recv_k = var_recv.at[k]
        tau_step = psteps[k]
        sigma_step = dsteps[k]

        for part in range(PIECES):
            for pair in range(part * group // 2, (part + 1) * group // 2):
                t = 2 * pair
                left = diagonal(w_tiles[row_s[0, t]], w_tiles[row_s[0, t + 1]])
                both = jnp.dot(
                    left,
                    blocks[pl.ds(t, 2)].reshape(2 * width, width),
                    preferred_element_type=F32,
                )
                keep(pair_row(t, part), both)
            span = pl.ds(part * piece, piece)
            terms_k[me, span] = prod[span, :].astype(BF16)

            @pl.when(chip < chips - 1)
            def _():
                chain_copy(k, chip, part, 0).start()

            @pl.when(chip > 0)
            def _():
                chain_copy(k, chip, part, 1).start()

        for part in range(PIECES):
            chain_copy(k, chip, part, 2).start()

        @pl.when(i == 0)
        def _():
            for offset in range(1, n_con):
                source = con_peer(offset)
                con_copy(idx, idx_send.at[offset - 1], idx_recv, source, source).wait_recv()
            lane = lax.broadcasted_iota(jnp.int32, (1, 2 * slots), 1)
            for pair in range(chips):
                both = jnp.where(
                    lane < slots, idx[2 * pair, 0:1, :], idx[2 * pair + 1, 0:1, :]
                )
                onehot[:, pl.ds(pair * 2 * slots, 2 * slots)] = (
                    lax.broadcasted_iota(jnp.int32, (col_tiles, 2 * slots), 0) == both
                ).astype(F32).astype(BF16)
            for offset in range(1, n_con):
                con_copy(
                    idx, idx_send.at[offset - 1], idx_recv, me, con_peer(offset)
                ).wait_send()

        for hop in range(1, chips):
            for part in range(PIECES):

                @pl.when(chip >= hop)
                def _():
                    arrived(k, me - 2 * hop, part)

                    @pl.when(chip < chips - 1)
                    def _():
                        chain_copy(k, chip - hop, part, 0).start()

                    chain_copy(k, chip - hop, part, 2).start()

                @pl.when(chip + hop < chips)
                def _():
                    arrived(k, me + 2 * hop, part)

                    @pl.when(chip > 0)
                    def _():
                        chain_copy(k, chip + hop, part, 1).start()

                    chain_copy(k, chip + hop, part, 2).start()

        for source in range(chips):
            for part in range(PIECES):
                arrived(k, source * 2 + 1 - core, part)

        @pl.when(i == 0)
        def _():
            load_saved(steps).wait()
            load_cot.wait()
            load_cost.wait()

        load_saved(k).wait()
        load_active(k).wait()

        def stacked(r):
            return jnp.concatenate(
                [
                    terms_k[d, pl.ds(part * piece + r * group, group), :]
                    for d in range(n_con)
                    for part in range(PIECES)
                ],
                axis=0,
            )

        for r in range(0, rhs, 2):
            spread = jnp.dot(
                onehot[...],
                jnp.concatenate([stacked(r), stacked(r + 1)], axis=1),
                preferred_element_type=F32,
            )
            p_tiles[pl.ds(r, col_tiles, stride=rhs), :] = spread[:, :width]
            p_tiles[pl.ds(r + 1, col_tiles, stride=rhs), :] = spread[:, width:]

        def columns(g, carry):
            for o in range(unroll):
                c = g * unroll + o
                cols = pl.ds(pl.multiple_of(c * width, width), width)
                rows = pl.ds(pl.multiple_of(c * rhs, rhs), rhs)
                p = p_tiles[rows, :]
                q = x_active[k, :, cols].astype(F32) * (
                    x_out[:, cols] - 2.0 * sigma_step * p
                )
                u_tiles[c] = q
                x_out[:, cols] = q + sigma_step * p
            return carry

        lax.fori_loop(0, col_tiles // unroll, columns, 0)

        @pl.when(k == 0)
        def _():
            store_x.start()

        for part in range(PIECES):
            for pair in range(part * group // 2, (part + 1) * group // 2):
                t = 2 * pair
                left = diagonal(u_tiles[col_s[0, t]], u_tiles[col_s[0, t + 1]])
                both = lax.dot_general(
                    left,
                    jnp.concatenate([blocks[t], blocks[t + 1]], axis=1),
                    (((1,), (1,)), ((), ())),
                    preferred_element_type=F32,
                )
                keep(pair_row(t, part), both)
        for r in range(rhs):
            slab = jnp.concatenate(
                [
                    prod[pl.ds(part * piece + r * group, group), :]
                    for part in range(PIECES)
                ],
                axis=0,
            )
            high = slab.astype(BF16)
            low = (slab - high.astype(F32)).astype(BF16)
            s_tiles[pl.ds(r, row_tiles, stride=rhs), :] = jnp.dot(
                row_onehot[...],
                jnp.concatenate([high, low], axis=0),
                preferred_element_type=F32,
            )
        row_terms_k[mine] = s_tiles[...].astype(BF16)
        for offset in range(1, n_var):
            var_copy(
                row_terms_k, var_send_k.at[offset - 1], var_recv_k, mine, var_peer(offset)
            ).start()

        def dual_dot(c, acc):
            cols = pl.ds(pl.multiple_of(c * width, width), width)
            rows = pl.ds(pl.multiple_of(c * rhs, rhs), rhs)
            return acc + s_tiles[rows, :] * y_saved[k, :, cols].astype(F32)

        def column_dots(g, accs):
            ext_acc, cost_acc = accs
            for o in range(unroll):
                c = g * unroll + o
                cols = pl.ds(pl.multiple_of(c * width, width), width)
                rows = pl.ds(pl.multiple_of(c * rhs, rhs), rhs)
                later = x_saved[k + 1, :, cols].astype(F32)
                earlier = x_saved[k, :, cols].astype(F32)
                ext_acc = ext_acc + p_tiles[rows, :] * (2.0 * later - earlier)
                cost_acc = cost_acc + u_tiles[c] * cost[:, cols]
            return ext_acc, cost_acc

        s_acc = lax.fori_loop(0, row_tiles, dual_dot, zeros, unroll=4)
        ext_acc, cost_acc = lax.fori_loop(
            0, col_tiles // unroll, column_dots, (zeros, zeros)
        )
        partial[pl.ds(k, 1), :] = jnp.sum(
            scale * s_acc - x_weight * cost_acc, axis=0, keepdims=True
        )
        partial[pl.ds(steps + k, 1), :] = jnp.sum(
            y_weight * w_acc - x_weight * ext_acc, axis=0, keepdims=True
        )

        @pl.when(k == 0)
        def _():
            g_con[me] = partial[...]
            for offset in range(1, n_con):
                con_copy(
                    g_con, gc_send.at[offset - 1], gc_recv, me, con_peer(offset)
                ).start()

        for offset in range(1, n_var):
            source = var_peer(offset)
            var_copy(
                row_terms_k, var_send_k.at[offset - 1], var_recv_k, source, source
            ).wait_recv()
        total = row_terms_k[0].astype(F32)
        for j in range(1, n_var):
            total = total + row_terms_k[j].astype(F32)
        s_tiles[...] = total
        before = jnp.maximum(k - 1, 0)

        def rows_loop(c, acc):
            cols = pl.ds(pl.multiple_of(c * width, width), width)
            rows = pl.ds(pl.multiple_of(c * rhs, rhs), rhs)
            y_bar = w_tiles[c] + tau_step * s_tiles[rows, :]
            y_out[:, cols] = y_bar
            w = y_active[before, :, cols].astype(F32) * y_bar
            w_tiles[c] = w
            return acc + w * demand[:, cols]

        w_acc = lax.fori_loop(0, row_tiles, rows_loop, zeros, unroll=8)

        for source in range(chips):
            for part in range(PIECES):

                @pl.when(jnp.logical_and(source <= chip, chip < chips - 1))
                def _():
                    chain_copy(k, source, part, 0).wait_send()

                @pl.when(jnp.logical_and(source >= chip, chip > 0))
                def _():
                    chain_copy(k, source, part, 1).wait_send()

                chain_copy(k, source, part, 2).wait_send()

        for offset in range(1, n_var):
            var_copy(
                row_terms_k, var_send_k.at[offset - 1], var_recv_k, mine, var_peer(offset)
            ).wait_send()
        return w_acc

    load_blocks.wait()
    lax.fori_loop(0, steps, step, w_acc)

    for offset in range(1, n_con):
        source = con_peer(offset)
        con_copy(g_con, gc_send.at[offset - 1], gc_recv, source, source).wait_recv()
    sums = g_con[0]
    for d in range(1, n_con):
        sums = sums + g_con[d]
    g_var[mine] = sums
    for offset in range(1, n_var):
        var_copy(g_var, gv_send.at[offset - 1], gv_recv, mine, var_peer(offset)).start()
    for offset in range(1, n_var):
        source = var_peer(offset)
        var_copy(g_var, gv_send.at[offset - 1], gv_recv, source, source).wait_recv()
    sums = g_var[0]
    for j in range(1, n_var):
        sums = sums + g_var[j]
    for n in range(2 * steps):
        g_out[n // steps, n % steps] = jnp.sum(sums[n : n + 1, :])
    for offset in range(1, n_con):
        con_copy(g_con, gc_send.at[offset - 1], gc_recv, me, con_peer(offset)).wait_send()
    for offset in range(1, n_var):
        var_copy(g_var, gv_send.at[offset - 1], gv_recv, mine, var_peer(offset)).wait_send()
    store_x.wait()


def per_device(
    tile_values,
    tile_row,
    tile_col,
    tile_count,
    unit_cost,
    demand,
    x_saved,
    y_saved,
    x_active,
    y_active,
    x_cot,
    y_cot,
    primal_step,
    dual_step,
):
    blocks = tile_values.reshape(tile_values.shape[2:])
    slots, width, _ = blocks.shape
    rhs = x_cot.shape[0]
    col_tiles = x_cot.shape[1] // width
    row_tiles = y_cot.shape[1] // width
    steps = primal_step.shape[0]
    n_con = lax.axis_size("con")
    n_var = lax.axis_size("var")
    chips = n_con // 2
    rows = tile_row.reshape(1, slots)
    cols = tile_col.reshape(1, slots)
    vmem = pl.BlockSpec(memory_space=pltpu.VMEM)
    smem = pl.BlockSpec(memory_space=pltpu.SMEM)
    hbm = pl.BlockSpec(memory_space=pl.ANY)
    dma = pltpu.SemaphoreType.DMA
    return pl.pallas_call(
        functools.partial(kernel, n_con, n_var),
        out_shape=(
            jax.ShapeDtypeStruct(x_cot.shape, F32),
            jax.ShapeDtypeStruct(y_cot.shape, F32),
            jax.ShapeDtypeStruct((2, steps), F32),
        ),
        in_specs=[smem] * 5
        + [vmem, vmem, hbm, hbm, vmem, hbm, vmem, hbm, vmem, hbm, vmem],
        out_specs=(hbm, vmem, smem),
        scratch_shapes=[
            pltpu.VMEM((slots, width, width), BF16),
            pltpu.VMEM((1, x_cot.shape[1]), F32),
            pltpu.VMEM(x_saved.shape, BF16),
            pltpu.VMEM(x_active.shape, jnp.int32),
            pltpu.VMEM(x_cot.shape, F32),
            dma((3,)),
            dma((steps + 1,)),
            dma((steps,)),
            dma((1,)),
            pltpu.VMEM((n_con, 8, 2 * slots), jnp.int32),
            pltpu.VMEM((col_tiles, n_con * slots), BF16),
            pltpu.VMEM((row_tiles, 2 * slots), BF16),
            pltpu.VMEM((rhs * slots, width), F32),
            pltpu.VMEM((steps, n_con, rhs * slots, width), BF16),
            pltpu.VMEM((steps, n_var, rhs * row_tiles, width), BF16),
            pltpu.VMEM((rhs * col_tiles, width), F32),
            pltpu.VMEM((col_tiles, rhs, width), F32),
            pltpu.VMEM((rhs * row_tiles, width), F32),
            pltpu.VMEM((row_tiles, rhs, width), F32),
            pltpu.VMEM((2 * steps, width), F32),
            pltpu.VMEM((n_con, 2 * steps, width), F32),
            pltpu.VMEM((n_var, 2 * steps, width), F32),
            dma((n_con - 1,)),
            dma((n_con,)),
            dma((steps, chips, PIECES, 3)),
            dma((steps, n_con, PIECES)),
            dma((steps, n_var - 1)),
            dma((steps, n_var)),
            dma((n_con - 1,)),
            dma((n_con,)),
            dma((n_var - 1,)),
            dma((n_var,)),
        ],
        compiler_params=pltpu.CompilerParams(
            collective_id=0, has_side_effects=True, vmem_limit_bytes=56 * 1024 * 1024
        ),
    )(
        rows,
        cols,
        tile_count.reshape(1, 1),
        primal_step,
        dual_step,
        rows,
        cols,
        blocks,
        unit_cost.reshape(1, unit_cost.shape[0]),
        demand,
        x_saved,
        y_saved,
        x_active,
        y_active,
        x_cot,
        y_cot,
    )


def solution(mesh):
    in_specs = (
        P("con", "var", "groups", None, None),
        P("con", "var", "groups"),
        P("con", "var", "groups"),
        P("con", "var", "groups"),
        P(("groups", "var")),
        P("groups", "con"),
        P(None, "groups", "var"),
        P(None, "groups", "con"),
        P(None, "groups", "var"),
        P(None, "groups", "con"),
        P("groups", "var"),
        P("groups", "con"),
        P(),
        P(),
    )
    out_specs = (P("groups", "var"), P("groups", "con"), P("groups", None))
    return jax.shard_map(
        per_device, mesh=mesh, in_specs=in_specs, out_specs=out_specs, check_vma=False
    )
```
